32 devices in a mesh: row: 4 (over y, core), col: 8 (over z, x).
Axes of the slice: x: 2, y: 2, z: 4, core: 2. Of those that a mesh axis runs over, the one named last changes fastest.
Arguments:
- amplitudes: bfloat16 [4096, 2048], P('row', 'col'), may hold values from -6 to 6
- drive: float32 [4096, 2048], P('row', 'col'), may hold values from -6 to 6
- pair_irrep: int32 [2048], replicated, may hold values from 0 to 7, as said below
- occ_irrep: int32 [4096], replicated, may hold values from 0 to 7
- ladder_ints: bfloat16 [2048, 2048], P('row', 'col'), may hold values from -0.375 to 0.375
- hole_ints: bfloat16 [4096, 4096], P('row'), may hold values from -0.25 to 0.25, as said below
- occ_energy: float32 [64], replicated, may hold values from -1.5 to -0.5
- pair_energy: float32 [2048], P('col'), may hold values from 1 to 3
Outputs:
- residual: float32 [4096, 2048], P('row', 'col')
- updated: bfloat16 [4096, 2048], P('row', 'col')
The draws below stay inside these ranges and needn't reach their ends.
Inputs may be any that keep to these rules, and one draw needn't show every extreme that they name: hole_ints is symmetric: hole_ints[ij, kl] == hole_ints[kl, ij]. `pair_irrep`: any irrep may hold any share of the virtual pairs, all of them included.
All inputs are finite; a program needn't handle non-finite values.
Results may differ from the reference program's by a relative error of at most 0.001.
Values may be sent and summed in bfloat16 or wider, within the bound.
A program may use at most 64 MiB of HBM per device.

```python
import jax
import jax.numpy as jnp

NOCC = 64
IRREPS = 8
OP = 4096
K = 2048
N_ROW = 4


def draw_hole_ints(key, part):
    key = jax.random.fold_in(key, 11)
    base_draw = jax.random.normal(key, (OP, OP), jnp.float32)
    scale_factor = jnp.sqrt(jnp.float32(IRREPS) / (2.0 * OP))
    summed = (base_draw + base_draw.T) * scale_factor
    return jnp.clip(summed, -0.25, 0.25).astype(jnp.bfloat16)


def orbital_labels(weight_key, pick_key):
    weights = jax.random.randint(weight_key, (IRREPS,), 1, 17)
    bounds = jnp.cumsum(weights).astype(jnp.int32)
    picks = jax.random.randint(pick_key, (K,), 0, bounds[IRREPS - 1])
    return jnp.sum((picks[:, None] >= bounds[None, :]).astype(jnp.int32), axis=1).astype(jnp.int32)


def draw_pair_irrep(key, part):
    key = jax.random.fold_in(key, 5)
    subkeys = jax.random.split(key, 6)
    first_orb = orbital_labels(subkeys[0], subkeys[1])
    second_orb = orbital_labels(subkeys[2], subkeys[3])
    labels = jnp.bitwise_xor(first_orb, second_orb)
    block_len = K // N_ROW
    chosen = jax.random.randint(subkeys[4], (), 0, N_ROW)
    filler = jax.random.randint(subkeys[5], (), 0, IRREPS)
    positions = jnp.arange(K, dtype=jnp.int32)
    labels = jnp.where(positions // block_len == chosen, filler, labels)
    return labels.astype(jnp.int32)


def plant(drawn, key, least, largest):
    longest = drawn.shape.index(max(drawn.shape))
    spots = []
    for shift in (0, 1):
        where = [jax.random.randint(jax.random.fold_in(key, axis), (), 0, length) for axis, length in enumerate(drawn.shape)]
        where[longest] = (where[longest] + shift) % drawn.shape[longest]
        spots.append(tuple(where))
    return drawn.at[spots[0]].set(least).at[spots[1]].set(largest)


def shard_levels(stream_key, dims, pieces, low, largest):
    def one(dim, parts):
        draws = jax.random.uniform(jax.random.fold_in(jax.random.fold_in(stream_key, 6), dim), (parts,), jnp.float32, low / len(pieces), largest / len(pieces))
        return jnp.repeat(jnp.exp(draws), dims[dim] // parts).reshape((-1,) + (1,) * (len(dims) - dim - 1))

    factor_of = one(*pieces[0])
    for cut in pieces[1:]:
        factor_of = factor_of * one(*cut)
    return factor_of


def normal_values(key, extent, width, most, pieces=(), kind=jnp.bfloat16):
    level = shard_levels(key, extent, pieces, -0.22, 0.18) if pieces else 1.0
    drawn = jax.random.normal(key, extent, jnp.float32) * width * level
    return jnp.minimum(jnp.maximum(drawn, -most), most).astype(kind)


def setup_inputs(seed: int = 0) -> dict:
    key_of = jax.random.split(jax.random.key(seed), 9)
    amplitudes = normal_values(key_of[0], (OP, K), 1.0, 6.0, ((0, 4), (1, 8)))
    drive = normal_values(key_of[1], (OP, K), 1.0, 6.0, ((0, 4), (1, 8)), jnp.float32)
    pair_irrep = draw_pair_irrep(jax.random.fold_in(key_of[8], 71), 0)
    occ_irrep = plant(jax.random.randint(key_of[3], (OP,), 0, IRREPS), jax.random.fold_in(key_of[3], 1), 0, IRREPS - 1).astype(jnp.int32)
    ladder_ints = normal_values(key_of[4], (K, K), (K // IRREPS) ** -0.5, 0.375, ((0, 4), (1, 8)))
    hole_ints = draw_hole_ints(jax.random.fold_in(key_of[8], 71), 0)
    occ_energy = jnp.clip(jax.random.uniform(key_of[6], (NOCC,), jnp.float32, -1.5, -0.5), -1.5, -0.5)
    pair_energy = jnp.clip(1.0 + 2.0 * jax.random.uniform(key_of[7], (K,), jnp.float32) ** shard_levels(key_of[7], (K,), ((0, 8),), -0.2, 0.2), 1.0, 3.0)
    return dict(amplitudes=amplitudes, drive=drive, pair_irrep=pair_irrep, occ_irrep=occ_irrep, ladder_ints=ladder_ints, hole_ints=hole_ints, occ_energy=occ_energy, pair_energy=pair_energy)


def reference(amplitudes, drive, pair_irrep, occ_irrep, ladder_ints, hole_ints, occ_energy, pair_energy):
    pair_keep = pair_irrep[:, None] == pair_irrep[None, :]
    ladder_sym = jnp.where(pair_keep, ladder_ints, jnp.zeros_like(ladder_ints))
    occ_keep = occ_irrep[:, None] == occ_irrep[None, :]
    hole_sym = jnp.where(occ_keep, hole_ints, jnp.zeros_like(hole_ints))
    particle = jnp.dot(amplitudes, ladder_sym, preferred_element_type=jnp.float32)
    hole_part = jnp.dot(hole_sym, amplitudes, preferred_element_type=jnp.float32)
    residual = drive + particle + hole_part
    pair_occ = (occ_energy[:, None] + occ_energy[None, :]).reshape(-1)
    denominator = pair_energy[None, :] - pair_occ[:, None]
    updated = (amplitudes.astype(jnp.float32) - residual / denominator).astype(jnp.bfloat16)
    return residual, updated
```

```python
import functools

import jax
import jax.numpy as jnp
from jax import lax
from jax.experimental import pallas as pl
from jax.experimental.pallas import tpu as pltpu
from jax.sharding import PartitionSpec as P

MESH = pl.DeviceIdType.MESH
WIRE = jnp.float32
CHUNKS = 4
LINE = 4
ROWS = 4


def kernel(
    a_ref, drive_ref, pair_ref, occ_ref, ladder_ref, hole_ref, energy_ref, pair_energy_ref,
    res_ref, upd_ref,
    zbuf, abuf, wbuf, wout, vbuf, occ_col, energy_col, psend, precv,
    v_sem, zs_sem, zr_sem, as_sem, ar_sem, ws_sem, wr_sem, wxs_sem, ps_sem, pr_sem,
):
    row = lax.axis_index("row")
    col = lax.axis_index("col")
    y, core = row // 2, row % 2
    z, x = col // 2, col % 2
    occ_rows, pair_cols = a_ref.shape
    step = occ_rows // CHUNKS
    sib = y * 2 + 1 - core
    ynb = (1 - y) * 2 + core
    diag = (1 - y) * 2 + 1 - core
    to_sib, to_y = (sib, col), (ynb, col)
    to_x = (row, z * 2 + 1 - x)
    to_right, to_left = (row, (z + 1) * 2 + x), (row, (z - 1) * 2 + x)

    def remote(src, dst, ssem, rsem, dev):
        return pltpu.make_async_remote_copy(
            src_ref=src, dst_ref=dst, send_sem=ssem, recv_sem=rsem, device_id=dev, device_id_type=MESH
        )

    def v_copy(rr):
        return pltpu.make_async_copy(
            hole_ref.at[:, pl.ds(pl.multiple_of(rr * occ_rows, occ_rows), occ_rows)], vbuf.at[rr], v_sem.at[rr]
        )

    for rr in (row, sib, ynb, diag):
        v_copy(rr).start()

    barrier = pltpu.get_barrier_semaphore()
    for dev in (to_sib, to_y, to_x):
        pl.semaphore_signal(barrier, inc=1, device_id=dev, device_id_type=MESH)

    @pl.when(z < LINE - 1)
    def _():
        pl.semaphore_signal(barrier, inc=1, device_id=to_right, device_id_type=MESH)

    @pl.when(z > 0)
    def _():
        pl.semaphore_signal(barrier, inc=1, device_id=to_left, device_id_type=MESH)

    zbuf[z] = a_ref[...]
    abuf[row] = a_ref[...]

    own_pairs = pair_ref[pl.ds(col, 1), :].astype(jnp.float32)
    for half in range(2):
        down = jnp.broadcast_to(
            pair_ref[pl.ds(row * 2 + half, 1), :].astype(jnp.float32), (pair_cols, pair_cols)
        ).T
        block = ladder_ref[half * pair_cols:(half + 1) * pair_cols, :].astype(jnp.float32)
        wout[half] = jnp.where(down == own_pairs, block, 0.0).astype(jnp.bfloat16)
    wbuf[row, x] = wout[x]

    pl.semaphore_wait(barrier, 3 + (z > 0).astype(jnp.int32) + (z < LINE - 1).astype(jnp.int32))

    def rows_of(k):
        return pl.ds(k * step, step)

    def z_copy(right, dist, k):
        src = z - dist if right else z + dist
        block = zbuf.at[src, rows_of(k), :]
        return remote(
            block, block, zs_sem.at[0 if right else 1, dist, k], zr_sem.at[src, k],
            to_right if right else to_left,
        )

    def z_recv(src, k):
        block = zbuf.at[src, rows_of(k), :]
        return remote(block, block, zs_sem.at[0, 0, k], zr_sem.at[src, k], to_right)

    def can_send(right, dist):
        if right:
            return jnp.logical_and(z - dist >= 0, z < LINE - 1)
        return jnp.logical_and(z + dist < LINE, z > 0)

    def z_send_own(k):
        for right in (True, False):
            @pl.when(can_send(right, 0))
            def _():
                z_copy(right, 0, k).start()

    def z_forward(dist, k):
        for right in (True, False):
            src = z - dist if right else z + dist
            here = src >= 0 if right else src < LINE

            @pl.when(here)
            def _():
                z_recv(src, k).wait_recv()

            @pl.when(can_send(right, dist))
            def _():
                z_copy(right, dist, k).start()

    z_send_own(0)

    w_x = remote(wout.at[1 - x], wbuf.at[row, x], wxs_sem, wr_sem.at[row, x], to_x)
    w_x.start()

    def w_copy(slot, part, dev, n):
        block = wbuf.at[slot, part]
        return remote(block, block, ws_sem.at[n], wr_sem.at[slot, part], dev)

    def a_copy(slot, dev, n):
        block = abuf.at[slot]
        return remote(block, block, as_sem.at[n], ar_sem.at[slot], dev)

    w_sends = [
        w_copy(row, x, to_y, 0), w_copy(row, x, to_sib, 1),
        w_copy(row, 1 - x, to_y, 2), w_copy(row, 1 - x, to_sib, 3),
        w_copy(ynb, x, to_sib, 4), w_copy(ynb, 1 - x, to_sib, 5),
    ]
    a_sends = [a_copy(row, to_y, 0), a_copy(row, to_sib, 1), a_copy(ynb, to_sib, 2)]
    w_sends[0].start()
    w_sends[1].start()
    a_sends[1].start()
    a_sends[0].start()
    z_send_own(1)

    occ_col[...] = jnp.broadcast_to(occ_ref[pl.ds(row, 1), :].astype(jnp.float32), (128, occ_rows)).T
    nocc = energy_ref.shape[0]

    def hole(rr, first):
        v_copy(rr).wait()

        @pl.loop(0, CHUNKS)
        def _(i):
            rows = pl.ds(pl.multiple_of(i * step, step), step)
            labels = occ_ref[pl.ds(rr, 1), :].astype(jnp.float32)
            keep = occ_col[rows, 0:1] == labels
            block = jnp.where(keep, vbuf[rr, rows, :].astype(jnp.float32), 0.0).astype(jnp.bfloat16)
            part = jnp.dot(block, abuf[rr], preferred_element_type=jnp.float32)
            if first:
                res_ref[rows, :] = drive_ref[rows, :] + part
            else:
                res_ref[rows, :] += part

    w_copy(row, 1 - x, to_y, 2).wait_recv()
    w_sends[2].start()
    w_sends[3].start()
    hole(row, True)
    z_forward(1, 0)
    w_sends[4].wait_recv()
    w_sends[4].start()
    a_copy(sib, to_sib, 1).wait_recv()
    hole(sib, False)
    z_forward(2, 0)
    z_send_own(2)
    w_sends[5].wait_recv()
    w_sends[5].start()
    z_forward(1, 1)
    a_sends[2].wait_recv()
    a_sends[2].start()
    z_forward(3, 0)
    hole(ynb, False)
    z_forward(2, 1)
    z_send_own(3)
    a_copy(diag, to_sib, 2).wait_recv()
    hole(diag, False)
    z_forward(3, 1)

    for slot, part, n in ((sib, x, 1), (sib, 1 - x, 3), (diag, x, 4), (diag, 1 - x, 5)):
        w_copy(slot, part, to_sib, n).wait_recv()

    def p_copy(k):
        return remote(psend.at[k], precv.at[k], ps_sem.at[k], pr_sem.at[k], to_x)

    def particle(k):
        rows = rows_of(k)
        away = jnp.zeros((step, pair_cols), jnp.float32)
        for s in range(LINE):
            away += jnp.dot(zbuf[s, rows, :], wbuf[s, 1 - x], preferred_element_type=jnp.float32)
        psend[k] = away.astype(WIRE)
        p_copy(k).start()
        own = res_ref[rows, :]
        for s in range(LINE):
            own += jnp.dot(zbuf[s, rows, :], wbuf[s, x], preferred_element_type=jnp.float32)
        res_ref[rows, :] = own

    def finish(k):
        p_copy(k).wait_recv()
        for i in range(step // nocc):
            base = k * step + i * nocc
            rows = pl.ds(base, nocc)
            total = res_ref[rows, :] + precv[k, pl.ds(i * nocc, nocc), :].astype(jnp.float32)
            res_ref[rows, :] = total
            first_energy = energy_ref[row * (occ_rows // nocc) + base // nocc]
            denominator = pair_energy_ref[...] - (energy_col[:, 0:1] + first_energy)
            upd_ref[rows, :] = (a_ref[rows, :].astype(jnp.float32) - total / denominator).astype(jnp.bfloat16)

    for i in range(nocc):
        energy_col[i:i + 1, :] = jnp.full((1, 128), energy_ref[i], jnp.float32)

    for k in range(CHUNKS):
        if k >= 2:
            for dist in (1, 2, 3):
                z_forward(dist, k)
        particle(k)
        if k >= 1:
            finish(k - 1)
    finish(CHUNKS - 1)

    for k in range(CHUNKS):
        p_copy(k).wait_send()
        for dist in range(LINE):
            for right in (True, False):
                @pl.when(can_send(right, dist))
                def _():
                    z_copy(right, dist, k).wait_send()
    w_x.wait_send()
    for copy in w_sends + a_sends:
        copy.wait_send()


def fused(amplitudes, drive, pair_irrep, occ_irrep, ladder_ints, hole_ints, occ_energy, pair_energy):
    occ_rows, pair_cols = amplitudes.shape
    step = occ_rows // CHUNKS
    pairs = pair_irrep.reshape(-1, pair_cols)
    occs = occ_irrep.reshape(-1, occ_rows)
    vmem = pl.BlockSpec(memory_space=pltpu.VMEM)
    dma = pltpu.SemaphoreType.DMA
    bf16 = jnp.bfloat16
    return pl.pallas_call(
        kernel,
        out_shape=(
            jax.ShapeDtypeStruct((occ_rows, pair_cols), jnp.float32),
            jax.ShapeDtypeStruct((occ_rows, pair_cols), bf16),
        ),
        in_specs=[vmem, vmem, vmem, vmem, vmem, pl.BlockSpec(memory_space=pl.ANY),
                  pl.BlockSpec(memory_space=pltpu.SMEM), vmem],
        out_specs=(vmem, vmem),
        scratch_shapes=[
            pltpu.VMEM((LINE, occ_rows, pair_cols), bf16),
            pltpu.VMEM((ROWS, occ_rows, pair_cols), bf16),
            pltpu.VMEM((ROWS, 2, pair_cols, pair_cols), bf16),
            pltpu.VMEM((2, pair_cols, pair_cols), bf16),
            pltpu.VMEM((ROWS, occ_rows, occ_rows), bf16),
            pltpu.VMEM((occ_rows, 128), jnp.float32),
            pltpu.VMEM((occ_energy.shape[0], 128), jnp.float32),
            pltpu.VMEM((CHUNKS, step, pair_cols), WIRE),
            pltpu.VMEM((CHUNKS, step, pair_cols), WIRE),
            dma((ROWS,)),
            dma((2, LINE, CHUNKS)), dma((LINE, CHUNKS)),
            dma((3,)), dma((ROWS,)),
            dma((6,)), dma((ROWS, 2)),
            dma,
            dma((CHUNKS,)), dma((CHUNKS,)),
        ],
        compiler_params=pltpu.CompilerParams(
            collective_id=0, has_side_effects=True, vmem_limit_bytes=48 * 2**20
        ),
        cost_estimate=pl.CostEstimate(flops=3_300_000_000, bytes_accessed=12_000_000, transcendentals=0),
    )(amplitudes, drive, pairs, occs, ladder_ints, hole_ints, occ_energy, pair_energy.reshape(1, -1))


def general(amplitudes, drive, pair_irrep, occ_irrep, ladder_ints, hole_ints, occ_energy, pair_energy):
    row_rank = lax.axis_index("row")
    col_rank = lax.axis_index("col")
    occ_rows = amplitudes.shape[0]
    pair_cols = amplitudes.shape[1]
    ladder_rows = ladder_ints.shape[0]
    own_pairs = lax.dynamic_slice_in_dim(pair_irrep, col_rank * pair_cols, pair_cols)
    ladder_labels = lax.dynamic_slice_in_dim(pair_irrep, row_rank * ladder_rows, ladder_rows)
    own_occ = lax.dynamic_slice_in_dim(occ_irrep, row_rank * occ_rows, occ_rows)
    ladder_kept = jnp.where(
        ladder_labels[:, None] == own_pairs[None, :], ladder_ints, jnp.zeros_like(ladder_ints)
    )
    ladder_full = lax.all_gather(ladder_kept, "row", axis=0, tiled=True)
    particle = jnp.dot(
        lax.all_gather(amplitudes, "col", axis=1, tiled=True),
        ladder_full,
        preferred_element_type=jnp.float32,
    )
    hole_kept = jnp.where(
        own_occ[:, None] == occ_irrep[None, :], hole_ints, jnp.zeros_like(hole_ints)
    )
    hole_part = jnp.dot(
        hole_kept,
        lax.all_gather(amplitudes, "row", axis=0, tiled=True),
        preferred_element_type=jnp.float32,
    )
    residual = drive + particle + hole_part
    pair_occ = (occ_energy[:, None] + occ_energy[None, :]).reshape(-1)
    own_energy = lax.dynamic_slice_in_dim(pair_occ, row_rank * occ_rows, occ_rows)
    denominator = pair_energy[None, :] - own_energy[:, None]
    updated = (amplitudes.astype(jnp.float32) - residual / denominator).astype(jnp.bfloat16)
    return (residual, updated)


def solution(mesh):
    body = fused if (mesh.shape["row"], mesh.shape["col"]) == (ROWS, 2 * LINE) else general
    in_specs = (
        P("row", "col"),
        P("row", "col"),
        P(),
        P(),
        P("row", "col"),
        P("row", None),
        P(),
        P("col"),
    )
    out_specs = (P("row", "col"), P("row", "col"))
    return jax.shard_map(body, mesh=mesh, in_specs=in_specs, out_specs=out_specs, check_vma=False)
```

```python
import functools

import jax
import jax.numpy as jnp
from jax import lax
from jax.experimental import pallas as pl
from jax.experimental.pallas import tpu as pltpu
from jax.sharding import PartitionSpec as P

MESH = pl.DeviceIdType.MESH
WIRE = jnp.float32
CHUNKS = 8
HALF = CHUNKS // 2
LINE = 4
ROWS = 4


def kernel(
    a_hbm, drive_hbm, pair_hbm, occ_hbm, ladder_hbm, hole_ref, energy_hbm, pair_energy_hbm,
    res_ref, upd_ref,
    zbuf, abuf, wbuf, wout, vbuf, occ_col, energy_col, psend, precv,
    pair_ref, occ_ref, ladder_ref, energy_ref, pair_energy_ref,
    v_sem, zs_sem, zr_sem, as_sem, ar_sem, ws_sem, wr_sem, wxs_sem, ps_sem, pr_sem, in_sem,
):
    row = lax.axis_index("row")
    col = lax.axis_index("col")
    y, core = row // 2, row % 2
    z, x = col // 2, col % 2
    occ_rows, pair_cols = a_hbm.shape
    step = occ_rows // CHUNKS
    sib = y * 2 + 1 - core
    ynb = (1 - y) * 2 + core
    diag = (1 - y) * 2 + 1 - core
    to_sib, to_y = (sib, col), (ynb, col)
    to_x = (row, z * 2 + 1 - x)
    to_right, to_left = (row, (z + 1) * 2 + x), (row, (z - 1) * 2 + x)

    def labels_of(ref, start, size):
        start = pl.multiple_of(start, size)
        return ref[pl.ds(start, size)].astype(jnp.float32).reshape(1, size)

    def remote(src, dst, ssem, rsem, dev):
        return pltpu.make_async_remote_copy(
            src_ref=src, dst_ref=dst, send_sem=ssem, recv_sem=rsem, device_id=dev, device_id_type=MESH
        )

    def v_copy(rr):
        return pltpu.make_async_copy(
            hole_ref.at[:, pl.ds(pl.multiple_of(rr * occ_rows, occ_rows), occ_rows)], vbuf.at[rr], v_sem.at[rr]
        )

    loads = [
        pltpu.make_async_copy(src, dst, in_sem.at[n])
        for n, (src, dst) in enumerate((
            (a_hbm, zbuf.at[z]), (a_hbm, abuf.at[row]), (ladder_hbm, ladder_ref), (pair_hbm, pair_ref),
            (occ_hbm, occ_ref), (drive_hbm, res_ref), (energy_hbm, energy_ref), (pair_energy_hbm, pair_energy_ref),
        ))
    ]
    for load in loads:
        load.start()
    for rr in (row, sib, ynb, diag):
        v_copy(rr).start()

    barrier = pltpu.get_barrier_semaphore()
    for dev in (to_sib, to_y, to_x):
        pl.semaphore_signal(barrier, inc=1, device_id=dev, device_id_type=MESH)

    @pl.when(z < LINE - 1)
    def _():
        pl.semaphore_signal(barrier, inc=1, device_id=to_right, device_id_type=MESH)

    @pl.when(z > 0)
    def _():
        pl.semaphore_signal(barrier, inc=1, device_id=to_left, device_id_type=MESH)

    loads[0].wait()
    loads[1].wait()
    pl.semaphore_wait(barrier, 3 + (z > 0).astype(jnp.int32) + (z < LINE - 1).astype(jnp.int32))

    def rows_of(k):
        return pl.ds(k * step, step)

    def z_copy(right, dist, k):
        src = z - dist if right else z + dist
        block = zbuf.at[src, rows_of(k), :]
        return remote(
            block, block, zs_sem.at[0 if right else 1, dist, k], zr_sem.at[src, k],
            to_right if right else to_left,
        )

    def z_recv(src, k):
        block = zbuf.at[src, rows_of(k), :]
        return remote(block, block, zs_sem.at[0, 0, k], zr_sem.at[src, k], to_right)

    def can_send(right, dist):
        if right:
            return jnp.logical_and(z - dist >= 0, z < LINE - 1)
        return jnp.logical_and(z + dist < LINE, z > 0)

    def z_send_own(k):
        for right in (True, False):
            @pl.when(can_send(right, 0))
            def _():
                z_copy(right, 0, k).start()

    def z_forward(dist, k):
        for right in (True, False):
            src = z - dist if right else z + dist
            here = src >= 0 if right else src < LINE

            @pl.when(here)
            def _():
                z_recv(src, k).wait_recv()

            @pl.when(can_send(right, dist))
            def _():
                z_copy(right, dist, k).start()

    for k in range(HALF + 2):
        z_send_own(k)

    def w_copy(slot, part, dev, n):
        block = wbuf.at[slot, part]
        return remote(block, block, ws_sem.at[n], wr_sem.at[slot, part], dev)

    def a_copy(slot, dev, n):
        block = abuf.at[slot]
        return remote(block, block, as_sem.at[n], ar_sem.at[slot], dev)

    w_sends = [
        w_copy(row, x, to_y, 0), w_copy(row, x, to_sib, 1),
        w_copy(row, 1 - x, to_y, 2), w_copy(row, 1 - x, to_sib, 3),
        w_copy(ynb, x, to_sib, 4), w_copy(ynb, 1 - x, to_sib, 5),
    ]
    a_sends = [a_copy(row, to_y, 0), a_copy(row, to_sib, 1), a_copy(ynb, to_sib, 2)]
    a_sends[0].start()
    a_sends[1].start()

    loads[2].wait()
    loads[3].wait()
    own_pairs = labels_of(pair_ref, col * pair_cols, pair_cols)
    for half in range(2):
        down = jnp.broadcast_to(
            labels_of(pair_ref, (row * 2 + half) * pair_cols, pair_cols), (pair_cols, pair_cols)
        ).T
        block = ladder_ref[half * pair_cols:(half + 1) * pair_cols, :].astype(jnp.float32)
        wout[half] = jnp.where(down == own_pairs, block, 0.0).astype(jnp.bfloat16)
    wbuf[row, x] = wout[x]
    w_x = remote(wout.at[1 - x], wbuf.at[row, x], wxs_sem, wr_sem.at[row, x], to_x)
    w_x.start()
    w_sends[0].start()
    w_sends[1].start()

    for load in loads[4:]:
        load.wait()
    occ_col[...] = jnp.broadcast_to(labels_of(occ_ref, row * occ_rows, occ_rows), (128, occ_rows)).T
    nocc = energy_ref.shape[0]

    tile = 256

    def hole(rr):
        v_copy(rr).wait()

        labels = labels_of(occ_ref, rr * occ_rows, occ_rows)

        @pl.loop(0, occ_rows // tile)
        def _(i):
            rows = pl.ds(pl.multiple_of(i * tile, tile), tile)
            keep = occ_col[rows, 0:1] == labels
            block = jnp.where(keep, vbuf[rr, rows, :].astype(jnp.float32), 0.0).astype(jnp.bfloat16)
            res_ref[rows, :] += jnp.dot(block, abuf[rr], preferred_element_type=jnp.float32)

    hole(row)
    w_copy(row, 1 - x, to_y, 2).wait_recv()
    w_sends[2].start()
    w_sends[3].start()
    for k in range(HALF):
        z_forward(1, k)
    a_copy(sib, to_sib, 1).wait_recv()
    hole(sib)
    for k in range(HALF):
        z_forward(2, k)
    for k in range(HALF + 2, CHUNKS):
        z_send_own(k)
    a_sends[2].wait_recv()
    a_sends[2].start()
    hole(ynb)
    for n in (4, 5):
        w_sends[n].wait_recv()
        w_sends[n].start()
    a_copy(diag, to_sib, 2).wait_recv()
    hole(diag)
    for k in (HALF, HALF + 1):
        z_forward(1, k)
    for slot, part, n in ((sib, x, 1), (sib, 1 - x, 3), (diag, x, 4), (diag, 1 - x, 5)):
        w_copy(slot, part, to_sib, n).wait_recv()

    def p_copy(k):
        return remote(psend.at[k], precv.at[k], ps_sem.at[k], pr_sem.at[k], to_x)

    def particle(k):
        rows = rows_of(k)
        away = jnp.zeros((step, pair_cols), jnp.float32)
        for s in range(LINE):
            away += jnp.dot(zbuf[s, rows, :], wbuf[s, 1 - x], preferred_element_type=jnp.float32)
        psend[k] = away.astype(WIRE)
        p_copy(k).start()
        own = res_ref[rows, :]
        for s in range(LINE):
            own += jnp.dot(zbuf[s, rows, :], wbuf[s, x], preferred_element_type=jnp.float32)
        res_ref[rows, :] = own

    def finish(k):
        p_copy(k).wait_recv()
        for i in range(step // nocc):
            base = k * step + i * nocc
            rows = pl.ds(base, nocc)
            total = res_ref[rows, :] + precv[k, pl.ds(i * nocc, nocc), :].astype(jnp.float32)
            res_ref[rows, :] = total
            first_energy = energy_ref[row * (occ_rows // nocc) + base // nocc]
            denominator = pair_energy_ref[...].reshape(1, pair_cols) - (energy_col[:, 0:1] + first_energy)
            upd_ref[rows, :] = (abuf[row, rows, :].astype(jnp.float32) - total / denominator).astype(jnp.bfloat16)

    for i in range(nocc):
        energy_col[i:i + 1, :] = jnp.full((1, 128), energy_ref[i], jnp.float32)

    for k in range(CHUNKS):
        if k >= HALF:
            z_forward(2, k)
            if k + 2 < CHUNKS:
                z_forward(1, k + 2)
        z_forward(3, k)
        particle(k)
        if k >= 1:
            finish(k - 1)
    finish(CHUNKS - 1)

    for k in range(CHUNKS):
        p_copy(k).wait_send()
        for dist in range(LINE):
            for right in (True, False):
                @pl.when(can_send(right, dist))
                def _():
                    z_copy(right, dist, k).wait_send()
    w_x.wait_send()
    for copy in w_sends + a_sends:
        copy.wait_send()


def fused(amplitudes, drive, pair_irrep, occ_irrep, ladder_ints, hole_ints, occ_energy, pair_energy):
    occ_rows, pair_cols = amplitudes.shape
    step = occ_rows // CHUNKS
    vmem = pl.BlockSpec(memory_space=pltpu.VMEM)
    dma = pltpu.SemaphoreType.DMA
    bf16 = jnp.bfloat16
    return pl.pallas_call(
        kernel,
        out_shape=(
            jax.ShapeDtypeStruct((occ_rows, pair_cols), jnp.float32),
            jax.ShapeDtypeStruct((occ_rows, pair_cols), bf16),
        ),
        in_specs=[pl.BlockSpec(memory_space=pl.ANY)] * 8,
        out_specs=(vmem, vmem),
        scratch_shapes=[
            pltpu.VMEM((LINE, occ_rows, pair_cols), bf16),
            pltpu.VMEM((ROWS, occ_rows, pair_cols), bf16),
            pltpu.VMEM((ROWS, 2, pair_cols, pair_cols), bf16),
            pltpu.VMEM((2, pair_cols, pair_cols), bf16),
            pltpu.VMEM((ROWS, occ_rows, occ_rows), bf16),
            pltpu.VMEM((occ_rows, 128), jnp.float32),
            pltpu.VMEM((occ_energy.shape[0], 128), jnp.float32),
            pltpu.VMEM((CHUNKS, step, pair_cols), WIRE),
            pltpu.VMEM((CHUNKS, step, pair_cols), WIRE),
            pltpu.VMEM(pair_irrep.shape, jnp.int32),
            pltpu.VMEM(occ_irrep.shape, jnp.int32),
            pltpu.VMEM(ladder_ints.shape, bf16),
            pltpu.SMEM(occ_energy.shape, jnp.float32),
            pltpu.VMEM(pair_energy.shape, jnp.float32),
            dma((ROWS,)),
            dma((2, LINE, CHUNKS)), dma((LINE, CHUNKS)),
            dma((3,)), dma((ROWS,)),
            dma((6,)), dma((ROWS, 2)),
            dma,
            dma((CHUNKS,)), dma((CHUNKS,)),
            dma((8,)),
        ],
        compiler_params=pltpu.CompilerParams(
            collective_id=0, has_side_effects=True, vmem_limit_bytes=58 * 2**20
        ),
        cost_estimate=pl.CostEstimate(flops=3_300_000_000, bytes_accessed=12_000_000, transcendentals=0),
    )(amplitudes, drive, pair_irrep, occ_irrep, ladder_ints, hole_ints, occ_energy, pair_energy)


def general(amplitudes, drive, pair_irrep, occ_irrep, ladder_ints, hole_ints, occ_energy, pair_energy):
    row_rank = lax.axis_index("row")
    col_rank = lax.axis_index("col")
    occ_rows = amplitudes.shape[0]
    pair_cols = amplitudes.shape[1]
    ladder_rows = ladder_ints.shape[0]
    own_pairs = lax.dynamic_slice_in_dim(pair_irrep, col_rank * pair_cols, pair_cols)
    ladder_labels = lax.dynamic_slice_in_dim(pair_irrep, row_rank * ladder_rows, ladder_rows)
    own_occ = lax.dynamic_slice_in_dim(occ_irrep, row_rank * occ_rows, occ_rows)
    ladder_kept = jnp.where(
        ladder_labels[:, None] == own_pairs[None, :], ladder_ints, jnp.zeros_like(ladder_ints)
    )
    ladder_full = lax.all_gather(ladder_kept, "row", axis=0, tiled=True)
    particle = jnp.dot(
        lax.all_gather(amplitudes, "col", axis=1, tiled=True),
        ladder_full,
        preferred_element_type=jnp.float32,
    )
    hole_kept = jnp.where(
        own_occ[:, None] == occ_irrep[None, :], hole_ints, jnp.zeros_like(hole_ints)
    )
    hole_part = jnp.dot(
        hole_kept,
        lax.all_gather(amplitudes, "row", axis=0, tiled=True),
        preferred_element_type=jnp.float32,
    )
    residual = drive + particle + hole_part
    pair_occ = (occ_energy[:, None] + occ_energy[None, :]).reshape(-1)
    own_energy = lax.dynamic_slice_in_dim(pair_occ, row_rank * occ_rows, occ_rows)
    denominator = pair_energy[None, :] - own_energy[:, None]
    updated = (amplitudes.astype(jnp.float32) - residual / denominator).astype(jnp.bfloat16)
    return (residual, updated)


def solution(mesh):
    body = fused if (mesh.shape["row"], mesh.shape["col"]) == (ROWS, 2 * LINE) else general
    in_specs = (
        P("row", "col"),
        P("row", "col"),
        P(),
        P(),
        P("row", "col"),
        P("row", None),
        P(),
        P("col"),
    )
    out_specs = (P("row", "col"), P("row", "col"))
    return jax.shard_map(body, mesh=mesh, in_specs=in_specs, out_specs=out_specs, check_vma=False)
```

```python
import functools

import jax
import jax.numpy as jnp
from jax import lax
from jax.experimental import pallas as pl
from jax.experimental.pallas import tpu as pltpu
from jax.sharding import PartitionSpec as P

MESH = pl.DeviceIdType.MESH
TAIL = 16
LEVELS = 32000.0
CHUNKS = 8
HALF = CHUNKS // 2
LINE = 4
ROWS = 4


def kernel(
    a_hbm, drive_hbm, pair_hbm, occ_hbm, ladder_hbm, hole_ref, energy_hbm, pair_energy_hbm,
    res_ref, upd_ref,
    zbuf, abuf, wbuf, wout, vbuf, occ_col, energy_col, qsend, qrecv, esend, erecv,
    pair_ref, occ_ref, ladder_ref, energy_ref, pair_energy_ref,
    v_sem, zs_sem, zr_sem, as_sem, ar_sem, ws_sem, wr_sem, wxs_sem, ps_sem, pr_sem, es_sem, er_sem, in_sem,
):
    row = lax.axis_index("row")
    col = lax.axis_index("col")
    y, core = row // 2, row % 2
    z, x = col // 2, col % 2
    occ_rows, pair_cols = a_hbm.shape
    step = occ_rows // CHUNKS
    sib = y * 2 + 1 - core
    ynb = (1 - y) * 2 + core
    diag = (1 - y) * 2 + 1 - core
    to_sib, to_y = (sib, col), (ynb, col)
    to_x = (row, z * 2 + 1 - x)
    middle = jnp.logical_or(z == 1, z == 2)
    end = jnp.logical_not(middle)
    mate, cross = (z // 2) * 2 + 1 - z % 2, 3 - z
    far = 3 - mate
    to_mate, to_cross = (row, mate * 2 + x), (row, cross * 2 + x)

    def labels_of(ref, start, size):
        start = pl.multiple_of(start, size)
        return ref[pl.ds(start, size)].astype(jnp.float32).reshape(1, size)

    def remote(src, dst, ssem, rsem, dev):
        return pltpu.make_async_remote_copy(
            src_ref=src, dst_ref=dst, send_sem=ssem, recv_sem=rsem, device_id=dev, device_id_type=MESH
        )

    def v_copy(rr):
        return pltpu.make_async_copy(
            hole_ref.at[:, pl.ds(pl.multiple_of(rr * occ_rows, occ_rows), occ_rows)], vbuf.at[rr], v_sem.at[rr]
        )

    loads = [
        pltpu.make_async_copy(src, dst, in_sem.at[n])
        for n, (src, dst) in enumerate((
            (a_hbm, zbuf.at[z]), (a_hbm, abuf.at[row]), (ladder_hbm, ladder_ref), (pair_hbm, pair_ref),
            (occ_hbm, occ_ref), (drive_hbm, res_ref), (energy_hbm, energy_ref), (pair_energy_hbm, pair_energy_ref),
        ))
    ]
    for load in loads:
        load.start()
    for rr in (row, sib, ynb, diag):
        v_copy(rr).start()

    barrier = pltpu.get_barrier_semaphore()
    for dev in (to_sib, to_y, to_x, to_mate):
        pl.semaphore_signal(barrier, inc=1, device_id=dev, device_id_type=MESH)

    @pl.when(middle)
    def _():
        pl.semaphore_signal(barrier, inc=1, device_id=to_cross, device_id_type=MESH)

    loads[0].wait()
    loads[1].wait()
    pl.semaphore_wait(barrier, 4 + middle.astype(jnp.int32))

    def rows_of(k):
        return pl.ds(k * step, step)

    def z_copy(src, k, dev, n):
        block = zbuf.at[src, rows_of(k), :]
        return remote(block, block, zs_sem.at[n, k], zr_sem.at[src, k], dev)

    def z_own(k):
        @pl.when(middle)
        def _():
            z_copy(z, k, to_cross, 0).start()

        @pl.when(end)
        def _():
            z_copy(z, k, to_mate, 0).start()

    def z_forward(k):
        z_copy(mate, k, to_cross, 1).wait_recv()
        z_copy(mate, k, to_cross, 1).start()

    for k in range(HALF + 1):
        z_own(k)

    def a_copy(slot, part, dev, n):
        size = occ_rows // 4
        block = abuf.at[slot, pl.ds(part * size, size), :]
        return remote(block, block, as_sem.at[n, part], ar_sem.at[slot, part], dev)

    def w_copy(group, slot, part, dev, n):
        block = wbuf.at[group, slot, part]
        return remote(block, block, ws_sem.at[group, n], wr_sem.at[group, slot, part], dev)

    def w_lift(part, n):
        return remote(wbuf.at[0, row, part], wbuf.at[1, row, part], ws_sem.at[0, n], wr_sem.at[1, row, part], to_mate)

    for part in range(4):
        a_copy(row, part, to_sib, 1).start()
    for part in range(2):
        a_copy(row, part, to_y, 0).start()

    loads[2].wait()
    loads[3].wait()
    own_pairs = labels_of(pair_ref, col * pair_cols, pair_cols)
    for half in range(2):
        down = jnp.broadcast_to(
            labels_of(pair_ref, (row * 2 + half) * pair_cols, pair_cols), (pair_cols, pair_cols)
        ).T
        block = ladder_ref[half * pair_cols:(half + 1) * pair_cols, :].astype(jnp.float32)
        wout[half] = jnp.where(down == own_pairs, block, 0.0).astype(jnp.bfloat16)
    wbuf[0, row, x] = wout[x]
    w_x = remote(wout.at[1 - x], wbuf.at[0, row, x], wxs_sem, wr_sem.at[0, row, x], to_x)
    w_x.start()
    parts = (x, 1 - x)

    def w_share(group, i):
        w_copy(group, row, parts[i], to_y, 3 * i).start()
        w_copy(group, row, parts[i], to_sib, 3 * i + 1).start()

    @pl.when(middle)
    def _():
        w_share(0, 0)

    @pl.when(end)
    def _():
        w_lift(x, 0).start()

    for load in loads[4:]:
        load.wait()
    occ_col[...] = jnp.broadcast_to(labels_of(occ_ref, row * occ_rows, occ_rows), (128, occ_rows)).T
    nocc = energy_ref.shape[0]

    tile = 256

    def hole(rr):
        v_copy(rr).wait()

        labels = labels_of(occ_ref, rr * occ_rows, occ_rows)

        @pl.loop(0, occ_rows // tile)
        def _(i):
            rows = pl.ds(pl.multiple_of(i * tile, tile), tile)
            keep = occ_col[rows, 0:1] == labels
            block = jnp.where(keep, vbuf[rr, rows, :].astype(jnp.float32), 0.0).astype(jnp.bfloat16)
            res_ref[rows, :] += jnp.dot(block, abuf[rr], preferred_element_type=jnp.float32)

    w_copy(0, row, 1 - x, to_y, 3).wait_recv()

    @pl.when(middle)
    def _():
        w_share(0, 1)

    @pl.when(end)
    def _():
        w_lift(1 - x, 1).start()

    hole(row)

    @pl.when(middle)
    def _():
        for i in range(2):
            w_copy(1, row, parts[i], to_y, 3 * i).wait_recv()
            w_share(1, i)
        for k in range(HALF):
            z_forward(k)

    for k in range(HALF + 1, CHUNKS):
        z_own(k)
    for part in range(2, 4):
        a_copy(row, part, to_y, 0).start()
    for part in range(4):
        a_copy(sib, part, to_sib, 1).wait_recv()
    hole(sib)

    @pl.when(middle)
    def _():
        for group in range(2):
            for i in range(2):
                w_copy(group, ynb, parts[i], to_sib, 3 * i + 2).wait_recv()
                w_copy(group, ynb, parts[i], to_sib, 3 * i + 2).start()
        for k in range(HALF, CHUNKS):
            z_forward(k)
        for group in range(2):
            for i in range(2):
                w_copy(group, sib, parts[i], to_sib, 3 * i + 1).wait_recv()
                w_copy(group, diag, parts[i], to_sib, 3 * i + 2).wait_recv()

    def encode(ref, total):
        most = jnp.max(jnp.abs(total), axis=0, keepdims=True)
        power = jnp.ceil(jnp.log2(jnp.maximum(most, 1e-30)))
        scaled = total * (LEVELS * jnp.exp2(-power))
        ref[0:step, :] = jnp.floor(scaled + 0.5).astype(jnp.int32).astype(jnp.int16)
        ref[step:step + TAIL, :] = jnp.broadcast_to(power, (TAIL, pair_cols)).astype(jnp.int32).astype(jnp.int16)

    def decode(ref, start, size):
        power = ref[step:step + TAIL, :].astype(jnp.int32).astype(jnp.float32)[0:1, :]
        block = ref[start:start + size, :].astype(jnp.int32).astype(jnp.float32)
        return block * (jnp.exp2(power) * (1.0 / LEVELS))

    def q_copy(k):
        return remote(qsend.at[k], qrecv.at[k], ps_sem.at[k], pr_sem.at[k], to_x)

    def q_pass(k):
        return remote(erecv.at[k, 1 - x], qrecv.at[k], ps_sem.at[k], pr_sem.at[k], to_x)

    def e_copy(k, part):
        return remote(esend.at[k, part], erecv.at[k, part], es_sem.at[k, part], er_sem.at[k, part], to_mate)

    def product(k, group, part):
        rows = rows_of(k)
        total = jnp.zeros((step, pair_cols), jnp.float32)
        for s in range(LINE):
            total += jnp.dot(zbuf[s, rows, :], wbuf[group, s, part], preferred_element_type=jnp.float32)
        return total

    def particle(k):
        rows = rows_of(k)

        @pl.when(middle)
        def _():
            z_copy(cross, k, to_cross, 0).wait_recv()
            z_copy(far, k, to_cross, 1).wait_recv()
            for part in (1 - x, x):
                encode(esend.at[k, part], product(k, 1, part))
                e_copy(k, part).start()
            encode(qsend.at[k], product(k, 0, 1 - x))
            q_copy(k).start()
            res_ref[rows, :] += product(k, 0, x)

        @pl.when(end)
        def _():
            e_copy(k, 1 - x).wait_recv()
            q_pass(k).start()
            e_copy(k, x).wait_recv()
            res_ref[rows, :] += decode(erecv.at[k, x], 0, step)

    def finish(k):
        q_copy(k).wait_recv()
        for i in range(step // nocc):
            base = k * step + i * nocc
            rows = pl.ds(base, nocc)
            total = res_ref[rows, :] + decode(qrecv.at[k], i * nocc, nocc)
            res_ref[rows, :] = total
            first_energy = energy_ref[row * (occ_rows // nocc) + base // nocc]
            denominator = pair_energy_ref[...].reshape(1, pair_cols) - (energy_col[:, 0:1] + first_energy)
            upd_ref[rows, :] = (abuf[row, rows, :].astype(jnp.float32) - total / denominator).astype(jnp.bfloat16)

    for i in range(nocc):
        energy_col[i:i + 1, :] = jnp.full((1, 128), energy_ref[i], jnp.float32)

    for k in range(CHUNKS):
        particle(k)
        if k == 1:
            for part in range(4):
                a_copy(ynb, part, to_sib, 2).wait_recv()
                a_copy(ynb, part, to_sib, 2).start()
            hole(ynb)
        if k == 3:
            for part in range(4):
                a_copy(diag, part, to_sib, 2).wait_recv()
            hole(diag)
        if k >= 4:
            finish(k - 4)
    for k in range(CHUNKS - 4, CHUNKS):
        finish(k)

    for part in range(4):
        a_copy(row, part, to_y, 0).wait_send()
        a_copy(row, part, to_sib, 1).wait_send()
        a_copy(ynb, part, to_sib, 2).wait_send()
    w_x.wait_send()

    @pl.when(middle)
    def _():
        for k in range(CHUNKS):
            z_copy(z, k, to_cross, 0).wait_send()
            z_copy(mate, k, to_cross, 1).wait_send()
            q_copy(k).wait_send()
            for part in range(2):
                e_copy(k, part).wait_send()
        for group in range(2):
            for i in range(2):
                w_copy(group, row, parts[i], to_y, 3 * i).wait_send()
                w_copy(group, row, parts[i], to_sib, 3 * i + 1).wait_send()
                w_copy(group, ynb, parts[i], to_sib, 3 * i + 2).wait_send()

    @pl.when(end)
    def _():
        for k in range(CHUNKS):
            z_copy(z, k, to_mate, 0).wait_send()
            q_pass(k).wait_send()
        w_lift(x, 0).wait_send()
        w_lift(1 - x, 1).wait_send()


def fused(amplitudes, drive, pair_irrep, occ_irrep, ladder_ints, hole_ints, occ_energy, pair_energy):
    occ_rows, pair_cols = amplitudes.shape
    step = occ_rows // CHUNKS
    vmem = pl.BlockSpec(memory_space=pltpu.VMEM)
    dma = pltpu.SemaphoreType.DMA
    bf16 = jnp.bfloat16
    return pl.pallas_call(
        kernel,
        out_shape=(
            jax.ShapeDtypeStruct((occ_rows, pair_cols), jnp.float32),
            jax.ShapeDtypeStruct((occ_rows, pair_cols), bf16),
        ),
        in_specs=[pl.BlockSpec(memory_space=pl.ANY)] * 8,
        out_specs=(vmem, vmem),
        scratch_shapes=[
            pltpu.VMEM((LINE, occ_rows, pair_cols), bf16),
            pltpu.VMEM((ROWS, occ_rows, pair_cols), bf16),
            pltpu.VMEM((2, ROWS, 2, pair_cols, pair_cols), bf16),
            pltpu.VMEM((2, pair_cols, pair_cols), bf16),
            pltpu.VMEM((ROWS, occ_rows, occ_rows), bf16),
            pltpu.VMEM((occ_rows, 128), jnp.float32),
            pltpu.VMEM((occ_energy.shape[0], 128), jnp.float32),
            pltpu.VMEM((CHUNKS, step + TAIL, pair_cols), jnp.int16),
            pltpu.VMEM((CHUNKS, step + TAIL, pair_cols), jnp.int16),
            pltpu.VMEM((CHUNKS, 2, step + TAIL, pair_cols), jnp.int16),
            pltpu.VMEM((CHUNKS, 2, step + TAIL, pair_cols), jnp.int16),
            pltpu.VMEM(pair_irrep.shape, jnp.int32),
            pltpu.VMEM(occ_irrep.shape, jnp.int32),
            pltpu.VMEM(ladder_ints.shape, bf16),
            pltpu.SMEM(occ_energy.shape, jnp.float32),
            pltpu.VMEM(pair_energy.shape, jnp.float32),
            dma((ROWS,)),
            dma((2, CHUNKS)), dma((LINE, CHUNKS)),
            dma((3, 4)), dma((ROWS, 4)),
            dma((2, 6)), dma((2, ROWS, 2)),
            dma,
            dma((CHUNKS,)), dma((CHUNKS,)),
            dma((CHUNKS, 2)), dma((CHUNKS, 2)),
            dma((8,)),
        ],
        compiler_params=pltpu.CompilerParams(
            collective_id=0, has_side_effects=True, vmem_limit_bytes=58 * 2**20
        ),
        cost_estimate=pl.CostEstimate(flops=3_300_000_000, bytes_accessed=12_000_000, transcendentals=0),
    )(amplitudes, drive, pair_irrep, occ_irrep, ladder_ints, hole_ints, occ_energy, pair_energy)


def general(amplitudes, drive, pair_irrep, occ_irrep, ladder_ints, hole_ints, occ_energy, pair_energy):
    row_rank = lax.axis_index("row")
    col_rank = lax.axis_index("col")
    occ_rows = amplitudes.shape[0]
    pair_cols = amplitudes.shape[1]
    ladder_rows = ladder_ints.shape[0]
    own_pairs = lax.dynamic_slice_in_dim(pair_irrep, col_rank * pair_cols, pair_cols)
    ladder_labels = lax.dynamic_slice_in_dim(pair_irrep, row_rank * ladder_rows, ladder_rows)
    own_occ = lax.dynamic_slice_in_dim(occ_irrep, row_rank * occ_rows, occ_rows)
    ladder_kept = jnp.where(
        ladder_labels[:, None] == own_pairs[None, :], ladder_ints, jnp.zeros_like(ladder_ints)
    )
    ladder_full = lax.all_gather(ladder_kept, "row", axis=0, tiled=True)
    particle = jnp.dot(
        lax.all_gather(amplitudes, "col", axis=1, tiled=True),
        ladder_full,
        preferred_element_type=jnp.float32,
    )
    hole_kept = jnp.where(
        own_occ[:, None] == occ_irrep[None, :], hole_ints, jnp.zeros_like(hole_ints)
    )
    hole_part = jnp.dot(
        hole_kept,
        lax.all_gather(amplitudes, "row", axis=0, tiled=True),
        preferred_element_type=jnp.float32,
    )
    residual = drive + particle + hole_part
    pair_occ = (occ_energy[:, None] + occ_energy[None, :]).reshape(-1)
    own_energy = lax.dynamic_slice_in_dim(pair_occ, row_rank * occ_rows, occ_rows)
    denominator = pair_energy[None, :] - own_energy[:, None]
    updated = (amplitudes.astype(jnp.float32) - residual / denominator).astype(jnp.bfloat16)
    return (residual, updated)


def solution(mesh):
    body = fused if (mesh.shape["row"], mesh.shape["col"]) == (ROWS, 2 * LINE) else general
    in_specs = (
        P("row", "col"),
        P("row", "col"),
        P(),
        P(),
        P("row", "col"),
        P("row", None),
        P(),
        P("col"),
    )
    out_specs = (P("row", "col"), P("row", "col"))
    return jax.shard_map(body, mesh=mesh, in_specs=in_specs, out_specs=out_specs, check_vma=False)
```

```python
import functools

import jax
import jax.numpy as jnp
from jax import lax
from jax.experimental import pallas as pl
from jax.experimental.pallas import tpu as pltpu
from jax.sharding import PartitionSpec as P

MESH = pl.DeviceIdType.MESH
TAIL = 16
LEVELS = 32000.0
CHUNKS = 8
HALF = CHUNKS // 2
WHOLE = 2
LINE = 4
ROWS = 4


def kernel(
    a_hbm, drive_hbm, pair_hbm, occ_hbm, ladder_hbm, hole_ref, energy_hbm, pair_energy_hbm,
    res_ref, upd_ref,
    zbuf, abuf, wbuf, wout, vbuf, occ_col, energy_col, qsend, qrecv, esend, erecv,
    pair_ref, occ_ref, ladder_ref, energy_ref, pair_energy_ref,
    v_sem, zs_sem, zr_sem, as_sem, ar_sem, ws_sem, wr_sem, wxs_sem, ps_sem, pr_sem, es_sem, er_sem, in_sem,
):
    row = lax.axis_index("row")
    col = lax.axis_index("col")
    y, core = row // 2, row % 2
    z, x = col // 2, col % 2
    occ_rows, pair_cols = a_hbm.shape
    step = occ_rows // CHUNKS
    sib = y * 2 + 1 - core
    ynb = (1 - y) * 2 + core
    diag = (1 - y) * 2 + 1 - core
    to_sib, to_y = (sib, col), (ynb, col)
    to_x = (row, z * 2 + 1 - x)
    middle = jnp.logical_or(z == 1, z == 2)
    end = jnp.logical_not(middle)
    mate, cross = (z // 2) * 2 + 1 - z % 2, 3 - z
    far = 3 - mate
    to_mate, to_cross = (row, mate * 2 + x), (row, cross * 2 + x)

    def labels_of(ref, start, size):
        start = pl.multiple_of(start, size)
        return ref[pl.ds(start, size)].astype(jnp.float32).reshape(1, size)

    def remote(src, dst, ssem, rsem, dev):
        return pltpu.make_async_remote_copy(
            src_ref=src, dst_ref=dst, send_sem=ssem, recv_sem=rsem, device_id=dev, device_id_type=MESH
        )

    def v_copy(rr):
        return pltpu.make_async_copy(
            hole_ref.at[:, pl.ds(pl.multiple_of(rr * occ_rows, occ_rows), occ_rows)], vbuf.at[rr], v_sem.at[rr]
        )

    loads = [
        pltpu.make_async_copy(src, dst, in_sem.at[n])
        for n, (src, dst) in enumerate((
            (a_hbm, zbuf.at[z]), (a_hbm, abuf.at[row]), (ladder_hbm, ladder_ref), (pair_hbm, pair_ref),
            (occ_hbm, occ_ref), (drive_hbm, res_ref), (energy_hbm, energy_ref), (pair_energy_hbm, pair_energy_ref),
        ))
    ]
    for load in loads:
        load.start()
    for rr in (row, sib, ynb, diag):
        v_copy(rr).start()

    barrier = pltpu.get_barrier_semaphore()
    for dev in (to_sib, to_y, to_x, to_mate):
        pl.semaphore_signal(barrier, inc=1, device_id=dev, device_id_type=MESH)

    @pl.when(middle)
    def _():
        pl.semaphore_signal(barrier, inc=1, device_id=to_cross, device_id_type=MESH)

    loads[0].wait()
    loads[1].wait()
    pl.semaphore_wait(barrier, 4 + middle.astype(jnp.int32))

    def rows_of(k):
        return pl.ds(k * step, step)

    def z_copy(src, k, dev, n):
        block = zbuf.at[src, rows_of(k), :]
        return remote(block, block, zs_sem.at[n, k], zr_sem.at[src, k], dev)

    def z_forward(k):
        z_copy(mate, k, to_cross, 1).wait_recv()
        z_copy(mate, k, to_cross, 1).start()

    @pl.when(middle)
    def _():
        for k in range(HALF + 1):
            z_copy(z, k, to_cross, 0).start()
        for k in range(WHOLE):
            z_copy(z, k, to_mate, 2).start()

    @pl.when(end)
    def _():
        for k in range(2):
            z_copy(z, k, to_mate, 0).start()

    def a_copy(slot, part, dev, n):
        size = occ_rows // 4
        block = abuf.at[slot, pl.ds(part * size, size), :]
        return remote(block, block, as_sem.at[n, part], ar_sem.at[slot, part], dev)

    def w_copy(group, slot, part, dev, n):
        block = wbuf.at[group, slot, part]
        return remote(block, block, ws_sem.at[group, n], wr_sem.at[group, slot, part], dev)

    def w_lift(slot, part, n):
        return remote(wbuf.at[0, slot, part], wbuf.at[1, slot, part], ws_sem.at[1, n], wr_sem.at[1, slot, part], to_mate)

    for part in range(4):
        a_copy(row, part, to_sib, 1).start()
    loads[2].wait()
    loads[3].wait()
    own_pairs = labels_of(pair_ref, col * pair_cols, pair_cols)
    for half in range(2):
        down = jnp.broadcast_to(
            labels_of(pair_ref, (row * 2 + half) * pair_cols, pair_cols), (pair_cols, pair_cols)
        ).T
        block = ladder_ref[half * pair_cols:(half + 1) * pair_cols, :].astype(jnp.float32)
        wout[half] = jnp.where(down == own_pairs, block, 0.0).astype(jnp.bfloat16)
    wbuf[0, row, x] = wout[x]
    w_x = remote(wout.at[1 - x], wbuf.at[0, row, x], wxs_sem, wr_sem.at[0, row, x], to_x)
    w_x.start()
    parts = (x, 1 - x)

    def w_share(group, i):
        w_copy(group, row, parts[i], to_y, 3 * i).start()
        w_copy(group, row, parts[i], to_sib, 3 * i + 1).start()

    w_share(0, 0)
    a_copy(row, 0, to_y, 0).start()

    @pl.when(end)
    def _():
        w_lift(row, x, 0).start()
        for k in range(2, 4):
            z_copy(z, k, to_mate, 0).start()

    for load in loads[4:]:
        load.wait()
    occ_col[...] = jnp.broadcast_to(labels_of(occ_ref, row * occ_rows, occ_rows), (128, occ_rows)).T
    nocc = energy_ref.shape[0]

    tile = 256

    def hole(rr):
        v_copy(rr).wait()

        labels = labels_of(occ_ref, rr * occ_rows, occ_rows)

        @pl.loop(0, occ_rows // tile)
        def _(i):
            rows = pl.ds(pl.multiple_of(i * tile, tile), tile)
            keep = occ_col[rows, 0:1].astype(jnp.bfloat16) == labels.astype(jnp.bfloat16)
            block = jnp.where(keep, vbuf[rr, rows, :], jnp.zeros((), jnp.bfloat16))
            res_ref[rows, :] += jnp.dot(block, abuf[rr], preferred_element_type=jnp.float32)

    w_copy(0, row, 1 - x, to_y, 3).wait_recv()
    w_share(0, 1)
    for part in range(1, 4):
        a_copy(row, part, to_y, 0).start()

    @pl.when(end)
    def _():
        w_lift(row, 1 - x, 1).start()

    hole(row)

    @pl.when(middle)
    def _():
        for k in range(HALF):
            z_forward(k)
        for k in range(WHOLE):
            z_copy(cross, k, to_mate, 3).wait_recv()
            z_copy(cross, k, to_mate, 3).start()
        for k in range(HALF + 1, CHUNKS):
            z_copy(z, k, to_cross, 0).start()

    for i in range(2):
        w_copy(0, ynb, parts[i], to_sib, 3 * i + 2).wait_recv()
        w_copy(0, ynb, parts[i], to_sib, 3 * i + 2).start()

    @pl.when(end)
    def _():
        for i in range(2):
            w_lift(ynb, parts[i], 2 + i).start()
        for k in range(4, CHUNKS):
            z_copy(z, k, to_mate, 0).start()

    @pl.when(middle)
    def _():
        for i in range(2):
            w_copy(1, row, parts[i], to_sib, i).wait_recv()
            w_copy(1, row, parts[i], to_sib, i).start()

    for part in range(4):
        a_copy(sib, part, to_sib, 1).wait_recv()
    hole(sib)

    @pl.when(middle)
    def _():
        for k in range(WHOLE):
            z_copy(far, k, to_mate, 4).wait_recv()
            z_copy(far, k, to_mate, 4).start()

    for i in range(2):
        w_copy(0, sib, parts[i], to_sib, 3 * i + 1).wait_recv()
        w_copy(0, diag, parts[i], to_sib, 3 * i + 2).wait_recv()

    def w_rest():
        for i in range(2):
            w_copy(1, ynb, parts[i], to_sib, 2 + i).wait_recv()
            w_copy(1, ynb, parts[i], to_sib, 2 + i).start()
        for slot, n in ((sib, 0), (diag, 2)):
            for i in range(2):
                w_copy(1, slot, parts[i], to_sib, n + i).wait_recv()

    def encode(ref, total):
        most = jnp.max(jnp.abs(total), axis=0, keepdims=True)
        power = jnp.ceil(jnp.log2(jnp.maximum(most, 1e-30)))
        scaled = total * (LEVELS * jnp.exp2(-power))
        ref[0:step, :] = jnp.floor(scaled + 0.5).astype(jnp.int32).astype(jnp.int16)
        ref[step:step + TAIL, :] = jnp.broadcast_to(power, (TAIL, pair_cols)).astype(jnp.int32).astype(jnp.int16)

    def decode(ref, start, size):
        power = ref[step:step + TAIL, :].astype(jnp.int32).astype(jnp.float32)[0:1, :]
        block = ref[start:start + size, :].astype(jnp.int32).astype(jnp.float32)
        return block * (jnp.exp2(power) * (1.0 / LEVELS))

    def q_copy(k):
        return remote(qsend.at[k], qrecv.at[k], ps_sem.at[k], pr_sem.at[k], to_x)

    def q_pass(k):
        return remote(erecv.at[k, 1 - x], qrecv.at[k], ps_sem.at[k], pr_sem.at[k], to_x)

    def e_copy(k, part):
        return remote(esend.at[k, part], erecv.at[k, part], es_sem.at[k, part], er_sem.at[k, part], to_mate)

    def product(k, group, part):
        rows = rows_of(k)
        total = jnp.zeros((step, pair_cols), jnp.float32)
        for s in range(LINE):
            total += jnp.dot(zbuf[s, rows, :], wbuf[group, s, part], preferred_element_type=jnp.float32)
        return total

    def particle(k):
        rows = rows_of(k)

        def share():
            encode(qsend.at[k], product(k, 0, 1 - x))
            q_copy(k).start()
            res_ref[rows, :] += product(k, 0, x)

        @pl.when(middle)
        def _():
            if k >= WHOLE:
                z_copy(cross, k, to_cross, 0).wait_recv()
                z_copy(far, k, to_cross, 1).wait_recv()
                for part in (1 - x, x):
                    encode(esend.at[k, part], product(k, 1, part))
                    e_copy(k, part).start()
            share()

        @pl.when(end)
        def _():
            if k < WHOLE:
                for src in (mate, far, 3 - z):
                    z_copy(src, k, to_mate, 0).wait_recv()
                share()
            else:
                e_copy(k, 1 - x).wait_recv()
                q_pass(k).start()
                e_copy(k, x).wait_recv()
                res_ref[rows, :] += decode(erecv.at[k, x], 0, step)

    def finish(k):
        q_copy(k).wait_recv()
        for i in range(step // nocc):
            base = k * step + i * nocc
            rows = pl.ds(base, nocc)
            total = res_ref[rows, :] + decode(qrecv.at[k], i * nocc, nocc)
            res_ref[rows, :] = total
            first_energy = energy_ref[row * (occ_rows // nocc) + base // nocc]
            denominator = pair_energy_ref[...].reshape(1, pair_cols) - (energy_col[:, 0:1] + first_energy)
            upd_ref[rows, :] = (abuf[row, rows, :].astype(jnp.float32) - total / denominator).astype(jnp.bfloat16)

    for i in range(nocc):
        energy_col[i:i + 1, :] = jnp.full((1, 128), energy_ref[i], jnp.float32)

    for k in range(CHUNKS):
        @pl.when(middle)
        def _():
            if k == WHOLE:
                w_rest()
            if 2 <= k < 6:
                z_forward(HALF + k - 2)

        particle(k)
        if k == 3:
            for part in range(4):
                a_copy(ynb, part, to_sib, 2).wait_recv()
                a_copy(ynb, part, to_sib, 2).start()
            hole(ynb)
        if k == 4:
            for part in range(4):
                a_copy(diag, part, to_sib, 2).wait_recv()
            hole(diag)
        if k >= 4:
            finish(k - 4)
    for k in range(CHUNKS - 4, CHUNKS):
        finish(k)

    for part in range(4):
        a_copy(row, part, to_y, 0).wait_send()
        a_copy(row, part, to_sib, 1).wait_send()
        a_copy(ynb, part, to_sib, 2).wait_send()
    w_x.wait_send()

    for k in range(CHUNKS):
        q_copy(k).wait_send()
    for i in range(2):
        w_copy(0, row, parts[i], to_y, 3 * i).wait_send()
        w_copy(0, row, parts[i], to_sib, 3 * i + 1).wait_send()
        w_copy(0, ynb, parts[i], to_sib, 3 * i + 2).wait_send()

    for n in range(4):
        w_copy(1, row, x, to_sib, n).wait_send()

    for k in range(CHUNKS):
        z_copy(z, k, to_mate, 0).wait_send()

    @pl.when(middle)
    def _():
        for k in range(CHUNKS):
            z_copy(mate, k, to_cross, 1).wait_send()
        for k in range(WHOLE):
            for n, src in ((2, z), (3, cross), (4, far)):
                z_copy(src, k, to_mate, n).wait_send()
        for k in range(WHOLE, CHUNKS):
            for part in range(2):
                e_copy(k, part).wait_send()


def fused(amplitudes, drive, pair_irrep, occ_irrep, ladder_ints, hole_ints, occ_energy, pair_energy):
    occ_rows, pair_cols = amplitudes.shape
    step = occ_rows // CHUNKS
    vmem = pl.BlockSpec(memory_space=pltpu.VMEM)
    dma = pltpu.SemaphoreType.DMA
    bf16 = jnp.bfloat16
    return pl.pallas_call(
        kernel,
        out_shape=(
            jax.ShapeDtypeStruct((occ_rows, pair_cols), jnp.float32),
            jax.ShapeDtypeStruct((occ_rows, pair_cols), bf16),
        ),
        in_specs=[pl.BlockSpec(memory_space=pl.ANY)] * 8,
        out_specs=(vmem, vmem),
        scratch_shapes=[
            pltpu.VMEM((LINE, occ_rows, pair_cols), bf16),
            pltpu.VMEM((ROWS, occ_rows, pair_cols), bf16),
            pltpu.VMEM((2, ROWS, 2, pair_cols, pair_cols), bf16),
            pltpu.VMEM((2, pair_cols, pair_cols), bf16),
            pltpu.VMEM((ROWS, occ_rows, occ_rows), bf16),
            pltpu.VMEM((occ_rows, 128), jnp.float32),
            pltpu.VMEM((occ_energy.shape[0], 128), jnp.float32),
            pltpu.VMEM((CHUNKS, step + TAIL, pair_cols), jnp.int16),
            pltpu.VMEM((CHUNKS, step + TAIL, pair_cols), jnp.int16),
            pltpu.VMEM((CHUNKS, 2, step + TAIL, pair_cols), jnp.int16),
            pltpu.VMEM((CHUNKS, 2, step + TAIL, pair_cols), jnp.int16),
            pltpu.VMEM(pair_irrep.shape, jnp.int32),
            pltpu.VMEM(occ_irrep.shape, jnp.int32),
            pltpu.VMEM(ladder_ints.shape, bf16),
            pltpu.SMEM(occ_energy.shape, jnp.float32),
            pltpu.VMEM(pair_energy.shape, jnp.float32),
            dma((ROWS,)),
            dma((5, CHUNKS)), dma((LINE, CHUNKS)),
            dma((3, 4)), dma((ROWS, 4)),
            dma((2, 6)), dma((2, ROWS, 2)),
            dma,
            dma((CHUNKS,)), dma((CHUNKS,)),
            dma((CHUNKS, 2)), dma((CHUNKS, 2)),
            dma((8,)),
        ],
        compiler_params=pltpu.CompilerParams(
            collective_id=0, has_side_effects=True, vmem_limit_bytes=58 * 2**20
        ),
        cost_estimate=pl.CostEstimate(flops=3_300_000_000, bytes_accessed=12_000_000, transcendentals=0),
    )(amplitudes, drive, pair_irrep, occ_irrep, ladder_ints, hole_ints, occ_energy, pair_energy)


def general(amplitudes, drive, pair_irrep, occ_irrep, ladder_ints, hole_ints, occ_energy, pair_energy):
    row_rank = lax.axis_index("row")
    col_rank = lax.axis_index("col")
    occ_rows = amplitudes.shape[0]
    pair_cols = amplitudes.shape[1]
    ladder_rows = ladder_ints.shape[0]
    own_pairs = lax.dynamic_slice_in_dim(pair_irrep, col_rank * pair_cols, pair_cols)
    ladder_labels = lax.dynamic_slice_in_dim(pair_irrep, row_rank * ladder_rows, ladder_rows)
    own_occ = lax.dynamic_slice_in_dim(occ_irrep, row_rank * occ_rows, occ_rows)
    ladder_kept = jnp.where(
        ladder_labels[:, None] == own_pairs[None, :], ladder_ints, jnp.zeros_like(ladder_ints)
    )
    ladder_full = lax.all_gather(ladder_kept, "row", axis=0, tiled=True)
    particle = jnp.dot(
        lax.all_gather(amplitudes, "col", axis=1, tiled=True),
        ladder_full,
        preferred_element_type=jnp.float32,
    )
    hole_kept = jnp.where(
        own_occ[:, None] == occ_irrep[None, :], hole_ints, jnp.zeros_like(hole_ints)
    )
    hole_part = jnp.dot(
        hole_kept,
        lax.all_gather(amplitudes, "row", axis=0, tiled=True),
        preferred_element_type=jnp.float32,
    )
    residual = drive + particle + hole_part
    pair_occ = (occ_energy[:, None] + occ_energy[None, :]).reshape(-1)
    own_energy = lax.dynamic_slice_in_dim(pair_occ, row_rank * occ_rows, occ_rows)
    denominator = pair_energy[None, :] - own_energy[:, None]
    updated = (amplitudes.astype(jnp.float32) - residual / denominator).astype(jnp.bfloat16)
    return (residual, updated)


def solution(mesh):
    body = fused if (mesh.shape["row"], mesh.shape["col"]) == (ROWS, 2 * LINE) else general
    in_specs = (
        P("row", "col"),
        P("row", "col"),
        P(),
        P(),
        P("row", "col"),
        P("row", None),
        P(),
        P("col"),
    )
    out_specs = (P("row", "col"), P("row", "col"))
    return jax.shard_map(body, mesh=mesh, in_specs=in_specs, out_specs=out_specs, check_vma=False)
```
